128 devices in a mesh: dp: 16 (over x, z_hi, core), fsdp: 8 (over z_lo, y).
Axes of the slice: x: 4, y: 4, z: 4 (z_hi: 2, z_lo: 2; z = z_hi * 2 + z_lo), core: 2. Of those that a mesh axis runs over, the one named last changes fastest.
Arguments:
- activations: bfloat16 [16384, 8192], P(('dp', 'fsdp')), may hold values from -24 to 24
- gate_cotangent: bfloat16 [16384, 28672], P(('dp', 'fsdp')), may hold values from -24 to 24
- up_cotangent: bfloat16 [16384, 28672], P(('dp', 'fsdp')), may hold values from -24 to 24
- seeds: int32 [2], replicated, may hold values from 0 to 999999
- gate_first: float32 [8192, 128], P('fsdp'), may hold values from -1.2 to 1.2
- gate_second: float32 [8192, 128], P('fsdp'), may hold values from 0.005 to 0.05
- up_first: float32 [8192, 128], P('fsdp'), may hold values from -1.2 to 1.2
- up_second: float32 [8192, 128], P('fsdp'), may hold values from 0.005 to 0.05
Outputs:
- gate_step: bfloat16 [8192, 28672], P('fsdp', 'dp')
- up_step: bfloat16 [8192, 28672], P('fsdp', 'dp')
- gate_first_new: float32 [8192, 128], P('fsdp')
- gate_second_new: float32 [8192, 128], P('fsdp')
- up_first_new: float32 [8192, 128], P('fsdp')
- up_second_new: float32 [8192, 128], P('fsdp')
The draws below stay inside these ranges and needn't reach their ends.
Inputs may be any that keep to these rules, and one draw needn't show every extreme that they name: seeds[0] is the gate projection's seed, seeds[1] the up projection's.
All inputs are finite; a program needn't handle non-finite values.
Results may differ from the reference program's by a relative error of at most 0.0063.
Values sent between devices are 32-bit elements; how exact they have to be, the bound alone decides.
No kernel may reach another device: no remote copies, remote signals or barrier semaphores. Data moves between devices by JAX's collectives and lax.ppermute only.
A program may use at most 128 MiB of HBM per device.

```python
import math
import jax
import jax.numpy as jnp
from jax import lax

D = 8192
FF = 28672
R = 128
TOKENS = 16384


def strengthened(array, stream_key, source, target, parts, factor):
    owner, partner = [(jnp.arange(array.shape[axis_at]) // (array.shape[axis_at] // parts)).reshape([-1 if axis == axis_at else 1 for axis in range(array.ndim)]) for axis_at in (source, target)]
    chosen = jax.random.permutation(stream_key, parts)[partner]
    strong = (owner == chosen) | (owner == (partner + parts // 2) % parts)
    return jnp.where(strong, factor * array, array)


def shard_levels(key, shape, cuts, low, high):
    def one(axis_at, shards_of):
        draws = jax.random.uniform(jax.random.fold_in(jax.random.fold_in(key, 6), axis_at), (shards_of,), jnp.float32, low / len(cuts), high / len(cuts))
        return jnp.repeat(jnp.exp(draws), shape[axis_at] // shards_of).reshape((-1,) + (1,) * (len(shape) - axis_at - 1))

    loudness = one(*cuts[0])
    for cut in cuts[1:]:
        loudness = loudness * one(*cut)
    return loudness


def scatter_about(own_key, dims, width, most, pieces=(), held_as=jnp.bfloat16):
    drawn = jax.random.normal(own_key, dims, jnp.float32) * width
    if len(pieces) > 0:
        drawn = shard_levels(own_key, dims, pieces, -0.22, 0.18) * drawn
    return jnp.clip(drawn, min=-most, max=most).astype(held_as)


def bell_draw_with(stream_key, extent, spread, most, pieces, heavy, kind=jnp.bfloat16):
    result = spread * jax.random.normal(stream_key, extent, jnp.float32)
    if pieces:
        result = result * shard_levels(stream_key, extent, pieces, -0.22, 0.18)
    return jnp.clip(strengthened(result, jax.random.fold_in(stream_key, 3), *heavy), -most, most).astype(kind)


def setup_inputs(seed: int = 0) -> dict:
    streams_of = jax.random.split(jax.random.key(seed), 9)
    activations = bell_draw_with(streams_of[0], (TOKENS, D), 1.0, 24.0, ((0, 128),), (0, 1, 128, 5.5))
    gate_cotangent = scatter_about(streams_of[1], (TOKENS, FF), 4.0, 24.0, ((0, 128),))
    up_cotangent = scatter_about(streams_of[2], (TOKENS, FF), 4.0, 24.0, ((0, 128),))
    seeds = jax.random.randint(streams_of[3], (2,), 0, 1000000).astype(jnp.int32)
    gate_first = scatter_about(streams_of[4], (D, R), 0.2, 1.2, ((0, 8),), jnp.float32)
    gate_second = jnp.clip(jnp.exp(math.log(0.05) - 2.3025851 * jax.random.uniform(streams_of[5], (D, R), jnp.float32) ** shard_levels(streams_of[5], (D, R), ((0, 8),), -0.2, 0.2)), 0.005, 0.05)
    up_first = scatter_about(streams_of[6], (D, R), 0.2, 1.2, ((0, 8),), jnp.float32)
    up_second = jnp.clip(jnp.exp(math.log(0.05) - 2.3025851 * jax.random.uniform(streams_of[7], (D, R), jnp.float32) ** shard_levels(streams_of[7], (D, R), ((0, 8),), -0.2, 0.2)), 0.005, 0.05)
    return dict(activations=activations, gate_cotangent=gate_cotangent, up_cotangent=up_cotangent, seeds=seeds, gate_first=gate_first, gate_second=gate_second, up_first=up_first, up_second=up_second)


beta_one = 0.9
beta_two = 0.95
bias_one = 1.0 - beta_one ** 10
bias_two = 1.0 - beta_two ** 10
epsilon = 1e-08

def projection(seed_value, rows, rank):
    index = lax.broadcasted_iota(jnp.int32, (rows, rank), 0) * rank + lax.broadcasted_iota(jnp.int32, (rows, rank), 1)
    mixed = jnp.bitwise_xor(index, seed_value)
    mixed = mixed * 668265261
    mixed = jnp.bitwise_xor(mixed, jnp.right_shift(mixed, 15) & 131071)
    mixed = mixed * 739982445
    mixed = jnp.bitwise_xor(mixed, jnp.right_shift(mixed, 12) & 1048575)
    level = jnp.right_shift(mixed, 8) & 65535
    unit = (level.astype(jnp.float32) + 0.5) * (2.0 / 65536.0) - 1.0
    return (unit * math.sqrt(3.0 / rank)).astype(jnp.bfloat16)

def one_weight(activations, cotangent, seed_value, first, second):
    basis = projection(seed_value, FF, R)
    reduced = jnp.dot(cotangent, basis, preferred_element_type=jnp.float32).astype(jnp.bfloat16)
    summed = lax.dot_general(activations, reduced, (((0,), (0,)), ((), ())), preferred_element_type=jnp.float32)
    grad = summed / TOKENS
    first_new = beta_one * first + (1.0 - beta_one) * grad
    second_new = beta_two * second + (1.0 - beta_two) * grad * grad
    direction = (first_new / bias_one / (jnp.sqrt(second_new / bias_two) + epsilon)).astype(jnp.bfloat16)
    weight_step = lax.dot_general(direction, basis, (((1,), (1,)), ((), ())), preferred_element_type=jnp.float32).astype(jnp.bfloat16)
    return (weight_step, first_new, second_new)

def reference(activations, gate_cotangent, up_cotangent, seeds, gate_first, gate_second, up_first, up_second):
    gate_step, gate_first_new, gate_second_new = one_weight(activations, gate_cotangent, seeds[0], gate_first, gate_second)
    up_step, up_first_new, up_second_new = one_weight(activations, up_cotangent, seeds[1], up_first, up_second)
    return (gate_step, up_step, gate_first_new, gate_second_new, up_first_new, up_second_new)
```

```python
import functools
import math

import jax
import jax.numpy as jnp
import numpy as np
from jax import lax
from jax.experimental import pallas as pl
from jax.experimental.pallas import tpu as pltpu
from jax.sharding import Mesh
from jax.sharding import PartitionSpec as P

FF = 28672
R = 128
TOKENS = 16384

beta_one = 0.9
beta_two = 0.95
bias_one = 1.0 - beta_one**10
bias_two = 1.0 - beta_two**10
epsilon = 1e-08

MIX_ONE = 668265261
MIX_TWO = 739982445
CENTRE = 32767.5 * 256.0
SCALE = float(np.float32(math.sqrt(3.0 / R))) * 2.0**-23

AXES = ("x", "zh", "core", "zl", "y")
SIZES = (4, 2, 2, 2, 4)

BF16 = jnp.bfloat16
F32 = jnp.float32


def finish(mixed):
    mixed = mixed ^ lax.shift_right_logical(mixed, 15)
    mixed = mixed * jnp.int32(MIX_TWO)
    mixed = mixed ^ lax.shift_right_logical(mixed, 12)
    level = (mixed & 0x00FFFF00).astype(F32)
    return ((level - CENTRE) * SCALE).astype(BF16)


def first_mix(local, low, seed):
    return (local ^ (seed & low)) * jnp.int32(MIX_ONE)


def base_mix(base, low, seed):
    return (base ^ (seed & ~low)) * jnp.int32(MIX_ONE)


CHUNK = 2048
TILE = 64
PIECE = 512


def reduce_kernel(
    seed_ref, gate_hbm, up_hbm, out_ref, gate_v, up_v, even, odd, acc, sems
):
    chunks = FF // CHUNK
    hbm = (gate_hbm, up_hbm)
    held = (gate_v, up_v)

    def copy(w, i):
        cols = pl.ds(pl.multiple_of(i * CHUNK, CHUNK), CHUNK)
        return pltpu.make_async_copy(hbm[w].at[:, cols], held[w].at[:, cols], sems.at[w, i])

    for i in range(chunks):
        for w in range(2):
            copy(w, i).start()
    low = TILE * R - 1
    local = lax.broadcasted_iota(jnp.int32, (TILE, R), 0) * R + lax.broadcasted_iota(
        jnp.int32, (TILE, R), 1
    )
    seeds = [seed_ref[0], seed_ref[1]]
    tables = [first_mix(local, low, seed) for seed in seeds]
    acc[...] = jnp.zeros_like(acc)

    def step(i, fill, use):
        if use is not None:
            for w in range(2):
                copy(w, i - 1).wait()
        for w in range(2):
            part = None
            for t in range(CHUNK // TILE):
                if fill is not None:
                    start = base_mix((i * CHUNK + t * TILE) * R, low, seeds[w])
                    fill[w, t * TILE : (t + 1) * TILE, :] = finish(tables[w] + start)
                if use is not None and (t + 1) * TILE % PIECE == 0:
                    d = (t + 1) * TILE - PIECE
                    cols = pl.ds(pl.multiple_of((i - 1) * CHUNK + d, PIECE), PIECE)
                    product = jnp.dot(
                        held[w][:, cols], use[w, d : d + PIECE, :], preferred_element_type=F32
                    )
                    part = product if part is None else part + product
            if part is not None:
                acc[w] += part

    step(0, even, None)

    def body(k, carry):
        step(2 * k + 1, odd, even)
        step(2 * k + 2, even, odd)
        return carry

    lax.fori_loop(0, chunks // 2 - 1, body, 0)
    step(chunks - 1, odd, even)
    step(chunks, None, odd)
    for w in range(2):
        out_ref[w] = acc[w].astype(BF16).astype(F32).T


def reduce_both(seeds, gate_cot, up_cot):
    rows = gate_cot.shape[0]
    return pl.pallas_call(
        reduce_kernel,
        in_specs=[
            pl.BlockSpec(memory_space=pltpu.SMEM),
            pl.BlockSpec(memory_space=pltpu.HBM),
            pl.BlockSpec(memory_space=pltpu.HBM),
        ],
        out_specs=pl.BlockSpec(memory_space=pltpu.VMEM),
        out_shape=jax.ShapeDtypeStruct((2, R, rows), F32),
        scratch_shapes=[
            pltpu.VMEM((rows, FF), BF16),
            pltpu.VMEM((rows, FF), BF16),
            pltpu.VMEM((2, CHUNK, R), BF16),
            pltpu.VMEM((2, CHUNK, R), BF16),
            pltpu.VMEM((2, rows, R), F32),
            pltpu.SemaphoreType.DMA((2, FF // CHUNK)),
        ],
        compiler_params=pltpu.CompilerParams(vmem_limit_bytes=50 * 2**20),
        cost_estimate=pl.CostEstimate(
            flops=4 * rows * FF * R, bytes_accessed=4 * rows * FF, transcendentals=0
        ),
        name="reduce_both",
    )(seeds, gate_cot, up_cot)


def place():
    return tuple(lax.axis_index(name).astype(jnp.int32) for name in AXES)


def pooled_columns(core, x, y, k, zl, j):
    zero = core == 0
    at = lax.rem(jnp.where(zero, x, y) + k, 4)
    a = zl * 4096 + j * jnp.where(zero, 1024, 128) + at * jnp.where(zero, 128, 1024)
    return pl.ds(pl.multiple_of(a + core * 512, 128), 128)


def theirs_kernel(act_ref, *outs):
    x, _, core, _, y = place()
    for k, out in enumerate(outs):
        for n in range(8):
            cols = pooled_columns(1 - core, x, y, k, n // 4, n % 4)
            out[:, n * 128 : (n + 1) * 128] = act_ref[:, cols].astype(F32)


def pairs_kernel(act_ref, *rest):
    x, _, core, _, y = place()
    for k, (far, out) in enumerate(zip(rest[:3], rest[3:])):
        rows = act_ref.shape[0]
        for n in range(8):
            cols = pooled_columns(core, x, y, k + 1, n // 4, n % 4)
            out[:rows, n * 128 : (n + 1) * 128] = act_ref[:, cols].astype(F32)
        out[rows:, :] = far[...]


def rows_for(kernel, name, height, count, act, *far):
    return pl.pallas_call(
        kernel,
        in_specs=[pl.BlockSpec(memory_space=pltpu.VMEM)] * (1 + len(far)),
        out_specs=[pl.BlockSpec(memory_space=pltpu.VMEM)] * count,
        out_shape=[jax.ShapeDtypeStruct((height, 1024), F32)] * count,
        compiler_params=pltpu.CompilerParams(vmem_limit_bytes=10 * 2**20),
        cost_estimate=pl.CostEstimate(
            flops=height * 8192, bytes_accessed=6 * 2**20, transcendentals=0
        ),
        name=name,
    )(act, *far)


def grad_kernel(act_ref, *rest):
    x, _, core, _, y = place()
    second_at = jnp.where(core == 0, y, x)
    others = rest[:4]
    reds = rest[4:8]
    outs = rest[8:12]
    left = jnp.concatenate(
        [
            jnp.concatenate(
                [red[side, w].astype(BF16) for red in reds for side in range(2)], axis=1
            )
            for w in range(2)
        ],
        axis=0,
    )
    for k in range(4):
        j = lax.rem(second_at + k, 4)
        columns = []
        for zl in range(2):
            b = zl * 512 + j * 128
            columns.append(
                jnp.concatenate(
                    [act_ref[:, pooled_columns(core, x, y, 0, zl, j)]]
                    + [
                        other[:, pl.ds(pl.multiple_of(b, 128), 128)].astype(BF16)
                        for other in others
                    ],
                    axis=0,
                )
            )
        product = jnp.dot(
            left, jnp.concatenate(columns, axis=1), preferred_element_type=F32
        )
        for zl in range(2):
            for w in range(2):
                outs[k][w, zl] = product[
                    w * 128 : (w + 1) * 128, zl * 128 : (zl + 1) * 128
                ]


def partial_grads(act, others, reds):
    return pl.pallas_call(
        grad_kernel,
        in_specs=[pl.BlockSpec(memory_space=pltpu.VMEM)] * 9,
        out_specs=[pl.BlockSpec(memory_space=pltpu.VMEM)] * 4,
        out_shape=[jax.ShapeDtypeStruct((2, 2, 128, 128), F32)] * 4,
        compiler_params=pltpu.CompilerParams(vmem_limit_bytes=16 * 2**20),
        cost_estimate=pl.CostEstimate(
            flops=2 * 256 * 1024 * 1024, bytes_accessed=6 * 2**20, transcendentals=0
        ),
        name="partial_grads",
    )(act, *others, *reds)


def columns_kernel(seed_ref, out_ref):
    x, zh, core, _, _ = place()
    low = 128 * R - 1
    local = lax.broadcasted_iota(jnp.int32, (R, 128), 1) * R + lax.broadcasted_iota(
        jnp.int32, (R, 128), 0
    )
    count = out_ref.shape[2]
    base = ((x * 2 + zh) * 2 + core) * count
    for w in range(2):
        seed = seed_ref[w]
        table = first_mix(local, low, seed)
        for t in range(count // 128):
            start = base_mix((base + t * 128) * R, low, seed)
            out_ref[w, :, t * 128 : (t + 1) * 128] = finish(table + start)


def basis_columns(seeds, count):
    return pl.pallas_call(
        columns_kernel,
        in_specs=[pl.BlockSpec(memory_space=pltpu.SMEM)],
        out_specs=pl.BlockSpec(memory_space=pltpu.VMEM),
        out_shape=jax.ShapeDtypeStruct((2, R, count), BF16),
        compiler_params=pltpu.CompilerParams(vmem_limit_bytes=4 * 2**20),
        cost_estimate=pl.CostEstimate(
            flops=40 * R * count, bytes_accessed=4 * R * count, transcendentals=0
        ),
        name="basis_columns",
    )(seeds)


def update_kernel(
    basis_ref, gf_ref, gs_ref, uf_ref, us_ref, *rest
):
    grads = rest[:8]
    step_out = rest[8:10]
    moment_out = rest[10:14]
    step_v = rest[14:16]
    moment_v = rest[16:20]
    sems = rest[20]
    firsts = (gf_ref, uf_ref)
    seconds = (gs_ref, us_ref)
    pending = []
    x, _, core, _, _ = place()
    for i in range(8):
        side = core if i < 4 else 1 - core
        start = (side * 4 + lax.rem(x - i % 4 + 4, 4)) * 128
        rows = pl.ds(pl.multiple_of(start, 128), 128)
        for w in range(2):
            grad = grads[i][w].T * (1.0 / TOKENS)
            first_new = beta_one * firsts[w][rows, :] + (1.0 - beta_one) * grad
            second_new = beta_two * seconds[w][rows, :] + (1.0 - beta_two) * grad * grad
            moment_v[2 * w][rows, :] = first_new
            moment_v[2 * w + 1][rows, :] = second_new
            direction = (
                first_new / bias_one / (jnp.sqrt(second_new / bias_two) + epsilon)
            ).astype(BF16)
            step_v[w][rows, :] = jnp.dot(
                direction, basis_ref[w], preferred_element_type=F32
            ).astype(BF16)
            n = 0
            for src, dst in (
                (step_v[w], step_out[w]),
                (moment_v[2 * w], moment_out[2 * w]),
                (moment_v[2 * w + 1], moment_out[2 * w + 1]),
            ):
                copy = pltpu.make_async_copy(src.at[rows, :], dst.at[rows, :], sems.at[i, w, n])
                copy.start()
                pending.append(copy)
                n += 1
    for copy in pending:
        copy.wait()


def update(basis, moments, grads):
    rows, cols = moments[0].shape[0], basis.shape[2]
    return pl.pallas_call(
        update_kernel,
        in_specs=[pl.BlockSpec(memory_space=pltpu.VMEM)] * 13,
        out_specs=[pl.BlockSpec(memory_space=pl.ANY)] * 6,
        out_shape=[jax.ShapeDtypeStruct((rows, cols), BF16)] * 2
        + [jax.ShapeDtypeStruct((rows, R), F32)] * 4,
        scratch_shapes=[pltpu.VMEM((rows, cols), BF16)] * 2
        + [pltpu.VMEM((rows, R), F32)] * 4
        + [pltpu.SemaphoreType.DMA((8, 2, 3))],
        compiler_params=pltpu.CompilerParams(vmem_limit_bytes=16 * 2**20),
        cost_estimate=pl.CostEstimate(
            flops=4 * rows * cols * R, bytes_accessed=12 * 2**20, transcendentals=0
        ),
        name="update",
    )(basis, *moments, *grads)


def send(value, to):
    perm = []
    for source in range(128):
        x, zh, core, zl, y = (int(v) for v in np.unravel_index(source, SIZES))
        nx, nz, ncore, ny = to(x, zh * 2 + zl, core, y)
        nz %= 4
        target = int(
            np.ravel_multi_index((nx % 4, nz // 2, ncore, nz % 2, ny % 4), SIZES)
        )
        perm.append((source, target))
    return lax.ppermute(value, AXES, perm)


def swap_core(value):
    return lax.ppermute(value, "core", [(0, 1), (1, 0)])


def local(act, gate_cot, up_cot, seeds, gate_first, gate_second, up_first, up_second):
    zl = lax.axis_index("zl")

    def pool(value, k):
        return send(value, lambda x, z, c, y: (x + k, z, c, y) if c == 0 else (x, z, c, y + k))

    def across(value, k):
        return send(value, lambda x, z, c, y: (x, z, c, y + k) if c == 0 else (x + k, z, c, y))

    rows = act.shape[0]
    swapped = [swap_core(v) for v in rows_for(theirs_kernel, "theirs", rows, 4, act)]
    pairs = rows_for(pairs_kernel, "pairs", 2 * rows, 3, act, *swapped[1:])
    moved = [pool(pairs[k - 1], k) for k in range(1, 4)]

    basis = basis_columns(seeds, FF // 16)

    late_seeds, pairs = lax.optimization_barrier((seeds, pairs))
    reduced = reduce_both(late_seeds, gate_cot, up_cot)
    pair = jnp.stack([reduced, swap_core(reduced)])
    pooled = [pool(pair, k) for k in (1, 2)]
    last, moved = lax.optimization_barrier((pair, moved))
    pooled.append(pool(last, 3))

    parts = partial_grads(act, [swapped[0]] + moved, [pair] + pooled)

    mine, basis = lax.optimization_barrier((parts[0], basis))
    for k in range(1, 4):
        mine = mine + across(parts[k], k)

    away = lax.dynamic_index_in_dim(mine, 1 - zl, 1, keepdims=False)
    here = lax.dynamic_index_in_dim(mine, zl, 1, keepdims=False)
    done = here + send(away, lambda x, z, c, y: (x, z + 1, c, y))
    done = done + send(away, lambda x, z, c, y: (x, z - 1, c, y))
    done = done + send(here, lambda x, z, c, y: (x, z + 2, c, y))

    own = [done] + [
        send(done, lambda x, z, c, y, k=k: (x + k, z, c, y)) for k in range(1, 4)
    ]
    theirs = [swap_core(piece) for piece in own]
    gate_step, up_step, gfn, gsn, ufn, usn = update(
        basis,
        (gate_first, gate_second, up_first, up_second),
        own + theirs,
    )
    return gate_step, up_step, gfn, gsn, ufn, usn


def solution(mesh):
    fine = Mesh(mesh.devices.reshape(SIZES), AXES)
    both = ("x", "zh", "core", "zl", "y")
    dp = ("x", "zh", "core")
    fsdp = ("zl", "y")
    return jax.shard_map(
        local,
        mesh=fine,
        in_specs=(P(both, None),) * 3 + (P(),) + (P(fsdp, None),) * 4,
        out_specs=(P(fsdp, dp),) * 2 + (P(fsdp, None),) * 4,
        check_vma=False,
    )
```

```python
import functools
import math

import jax
import jax.numpy as jnp
import numpy as np
from jax import lax
from jax.experimental import pallas as pl
from jax.experimental.pallas import tpu as pltpu
from jax.sharding import Mesh
from jax.sharding import PartitionSpec as P

FF = 28672
R = 128
TOKENS = 16384

beta_one = 0.9
beta_two = 0.95
bias_one = 1.0 - beta_one**10
bias_two = 1.0 - beta_two**10
epsilon = 1e-08

MIX_ONE = 668265261
MIX_TWO = 739982445
CENTRE = 32767.5 * 256.0
SCALE = float(np.float32(math.sqrt(3.0 / R))) * 2.0**-23

AXES = ("x", "zh", "core", "zl", "y")
SIZES = (4, 2, 2, 2, 4)

BF16 = jnp.bfloat16
F32 = jnp.float32


def finish(mixed):
    mixed = mixed ^ lax.shift_right_logical(mixed, 15)
    mixed = mixed * jnp.int32(MIX_TWO)
    mixed = mixed ^ lax.shift_right_logical(mixed, 12)
    level = (mixed & 0x00FFFF00).astype(F32)
    return ((level - CENTRE) * SCALE).astype(BF16)


def first_mix(local, low, seed):
    return (local ^ (seed & low)) * jnp.int32(MIX_ONE)


def base_mix(base, low, seed):
    return (base ^ (seed & ~low)) * jnp.int32(MIX_ONE)


CHUNK = 4096
TILE = 64
PIECE = 512
LOW = TILE * R - 1
FIRST, LAST = 0, 115


def tile_table(seed):
    local = lax.broadcasted_iota(jnp.int32, (TILE, R), 0) * R + lax.broadcasted_iota(
        jnp.int32, (TILE, R), 1
    )
    return first_mix(local, LOW, seed)


def basis_tile(table, seed, row):
    return finish(table + base_mix(row * R, LOW, seed))


def reduce_kernel(
    seed_ref, gate_hbm, up_hbm, out_ref, gate_v, up_v, even, odd, acc, sems
):
    chunks = FF // CHUNK
    hbm = (gate_hbm, up_hbm)
    held = (gate_v, up_v)

    def copy(w, i):
        cols = pl.ds(pl.multiple_of(i * CHUNK, CHUNK), CHUNK)
        return pltpu.make_async_copy(hbm[w].at[:, cols], held[w].at[:, cols], sems.at[w, i])

    for i in range(chunks):
        for w in range(2):
            copy(w, i).start()
    seeds = [seed_ref[0], seed_ref[1]]
    tables = [tile_table(seed) for seed in seeds]
    acc[...] = jnp.zeros_like(acc)
    tiles = [(w, t) for w in range(2) for t in range(0, CHUNK, TILE)]
    pieces = [(w, d) for w in range(2) for d in range(0, CHUNK, PIECE)]
    due = [
        max(0, min(len(pieces), -(-(n - FIRST) * len(pieces) // (LAST - FIRST))))
        for n in range(len(tiles))
    ]

    def step(i, fill, use):
        parts = [None, None]

        def multiply(w, d):
            if d == 0:
                copy(w, i - 1).wait()
            cols = pl.ds(pl.multiple_of((i - 1) * CHUNK + d, PIECE), PIECE)
            product = jnp.dot(
                held[w][:, cols], use[w, d : d + PIECE, :], preferred_element_type=F32
            )
            parts[w] = product if parts[w] is None else parts[w] + product

        if fill is None:
            for piece in pieces:
                multiply(*piece)
        else:
            done = 0
            for n, (w, t) in enumerate(tiles):
                for piece in pieces[done : due[n]]:
                    multiply(*piece)
                done = due[n]
                fill[w, t : t + TILE, :] = basis_tile(tables[w], seeds[w], i * CHUNK + t)
        for w in range(2):
            acc[w] += parts[w]

    for w, t in tiles:
        even[w, t : t + TILE, :] = basis_tile(tables[w], seeds[w], t)

    def body(k, carry):
        step(2 * k + 1, odd, even)
        step(2 * k + 2, even, odd)
        return carry

    lax.fori_loop(0, chunks // 2, body, 0)
    step(chunks, None, even)
    for w in range(2):
        out_ref[w] = acc[w].astype(BF16).astype(F32).T


def reduce_both(seeds, gate_cot, up_cot):
    rows = gate_cot.shape[0]
    return pl.pallas_call(
        reduce_kernel,
        in_specs=[
            pl.BlockSpec(memory_space=pltpu.SMEM),
            pl.BlockSpec(memory_space=pltpu.HBM),
            pl.BlockSpec(memory_space=pltpu.HBM),
        ],
        out_specs=pl.BlockSpec(memory_space=pltpu.VMEM),
        out_shape=jax.ShapeDtypeStruct((2, R, rows), F32),
        scratch_shapes=[
            pltpu.VMEM((rows, FF), BF16),
            pltpu.VMEM((rows, FF), BF16),
            pltpu.VMEM((2, CHUNK, R), BF16),
            pltpu.VMEM((2, CHUNK, R), BF16),
            pltpu.VMEM((2, rows, R), F32),
            pltpu.SemaphoreType.DMA((2, FF // CHUNK)),
        ],
        compiler_params=pltpu.CompilerParams(vmem_limit_bytes=50 * 2**20),
        cost_estimate=pl.CostEstimate(
            flops=20 * rows * FF * R, bytes_accessed=4 * rows * FF, transcendentals=0
        ),
        name="reduce_both",
    )(seeds, gate_cot, up_cot)


def place():
    return tuple(lax.axis_index(name).astype(jnp.int32) for name in AXES)


def pooled_columns(core, x, y, k, zl, j):
    zero = core == 0
    at = lax.rem(jnp.where(zero, x, y) + k, 4)
    a = zl * 4096 + j * jnp.where(zero, 1024, 128) + at * jnp.where(zero, 128, 1024)
    return pl.ds(pl.multiple_of(a + core * 512, 128), 128)


def theirs_kernel(act_ref, *outs):
    x, _, core, _, y = place()
    for i, out in enumerate(outs):
        owner, k = (1 - core, i) if i < 4 else (core, 2)
        for n in range(8):
            cols = pooled_columns(owner, x, y, k, n // 4, n % 4)
            out[:, n * 128 : (n + 1) * 128] = act_ref[:, cols].astype(F32)


def pair_kernel(act_ref, far_ref, out_ref, *, k):
    x, _, core, _, y = place()
    rows = act_ref.shape[0]
    for n in range(8):
        cols = pooled_columns(core, x, y, k, n // 4, n % 4)
        out_ref[:rows, n * 128 : (n + 1) * 128] = act_ref[:, cols].astype(F32)
    out_ref[rows:, :] = far_ref[...]


def rows_for(kernel, name, height, count, act, *far):
    return pl.pallas_call(
        kernel,
        in_specs=[pl.BlockSpec(memory_space=pltpu.VMEM)] * (1 + len(far)),
        out_specs=[pl.BlockSpec(memory_space=pltpu.VMEM)] * count,
        out_shape=[jax.ShapeDtypeStruct((height, 1024), F32)] * count,
        compiler_params=pltpu.CompilerParams(vmem_limit_bytes=10 * 2**20),
        cost_estimate=pl.CostEstimate(
            flops=height * 8192, bytes_accessed=6 * 2**20, transcendentals=0
        ),
        name=name,
    )(act, *far)


def grad_kernel(act_ref, *rest):
    x, _, core, _, y = place()
    second_at = jnp.where(core == 0, y, x)
    others = rest[:5]
    reds = rest[5:9]
    outs = rest[9:13]
    left = jnp.concatenate(
        [
            jnp.concatenate(
                [red[side, w].astype(BF16) for red in reds for side in range(2)], axis=1
            )
            for w in range(2)
        ],
        axis=0,
    )
    for k in range(4):
        j = lax.rem(second_at + k, 4)
        columns = []
        for zl in range(2):
            b = zl * 512 + j * 128
            columns.append(
                jnp.concatenate(
                    [act_ref[:, pooled_columns(core, x, y, 0, zl, j)]]
                    + [
                        other[:, pl.ds(pl.multiple_of(b, 128), 128)].astype(BF16)
                        for other in others
                    ],
                    axis=0,
                )
            )
        product = jnp.dot(
            left, jnp.concatenate(columns, axis=1), preferred_element_type=F32
        )
        for zl in range(2):
            for w in range(2):
                outs[k][w, zl] = product[
                    w * 128 : (w + 1) * 128, zl * 128 : (zl + 1) * 128
                ]


def partial_grads(act, others, reds):
    return pl.pallas_call(
        grad_kernel,
        in_specs=[pl.BlockSpec(memory_space=pltpu.VMEM)] * 10,
        out_specs=[pl.BlockSpec(memory_space=pltpu.VMEM)] * 4,
        out_shape=[jax.ShapeDtypeStruct((2, 2, 128, 128), F32)] * 4,
        compiler_params=pltpu.CompilerParams(vmem_limit_bytes=16 * 2**20),
        cost_estimate=pl.CostEstimate(
            flops=2 * 256 * 1024 * 1024, bytes_accessed=6 * 2**20, transcendentals=0
        ),
        name="partial_grads",
    )(act, *others, *reds)


def sum_kernel(*refs):
    zl = lax.axis_index("zl").astype(jnp.int32)
    here_ref, away_ref = refs[4:]
    for ref, at in ((here_ref, zl), (away_ref, 1 - zl)):
        for w in range(2):
            ref[w] = (refs[0][w, at] + refs[1][w, at]) + (refs[2][w, at] + refs[3][w, at])


def sum_second(parts):
    return pl.pallas_call(
        sum_kernel,
        in_specs=[pl.BlockSpec(memory_space=pltpu.VMEM)] * 4,
        out_specs=[pl.BlockSpec(memory_space=pltpu.VMEM)] * 2,
        out_shape=[jax.ShapeDtypeStruct((2, 128, 128), F32)] * 2,
        compiler_params=pltpu.CompilerParams(vmem_limit_bytes=4 * 2**20),
        cost_estimate=pl.CostEstimate(flops=10**6, bytes_accessed=10**6, transcendentals=0),
        name="sum_second",
    )(*parts)


def columns_kernel(seed_ref, out_ref):
    x, zh, core, _, _ = place()
    low = 128 * R - 1
    local = lax.broadcasted_iota(jnp.int32, (R, 128), 1) * R + lax.broadcasted_iota(
        jnp.int32, (R, 128), 0
    )
    count = out_ref.shape[2]
    base = ((x * 2 + zh) * 2 + core) * count
    for w in range(2):
        seed = seed_ref[w]
        table = first_mix(local, low, seed)
        for t in range(count // 128):
            start = base_mix((base + t * 128) * R, low, seed)
            out_ref[w, :, t * 128 : (t + 1) * 128] = finish(table + start)


def basis_columns(seeds, count):
    return pl.pallas_call(
        columns_kernel,
        in_specs=[pl.BlockSpec(memory_space=pltpu.SMEM)],
        out_specs=pl.BlockSpec(memory_space=pltpu.VMEM),
        out_shape=jax.ShapeDtypeStruct((2, R, count), BF16),
        compiler_params=pltpu.CompilerParams(vmem_limit_bytes=4 * 2**20),
        cost_estimate=pl.CostEstimate(
            flops=40 * R * count, bytes_accessed=4 * R * count, transcendentals=0
        ),
        name="basis_columns",
    )(seeds)


def update_kernel(basis_ref, gf_ref, gs_ref, uf_ref, us_ref, *rest, places, before):
    count = len(places)
    grads = rest[:count]
    outs = rest[count + before : count + before + 6]
    step_v, moment_v, direction_v, sems = rest[count + before + 6 :]
    firsts = (gf_ref, uf_ref)
    seconds = (gs_ref, us_ref)
    pending = []
    x, _, core, _, _ = place()
    starts = []
    for k, other in places:
        side = 1 - core if other else core
        starts.append(pl.multiple_of((side * 4 + lax.rem(x - k + 4, 4)) * 128, 128))

    def send_out(src, dst, start, sem):
        copy = pltpu.make_async_copy(src, dst.at[pl.ds(start, 128), :], sem)
        copy.start()
        pending.append(copy)

    for w in range(2):
        for i, start in enumerate(starts):
            rows = pl.ds(start, 128)
            here = pl.ds(i * 128, 128)
            grad = grads[i][w].T * (1.0 / TOKENS)
            first_new = beta_one * firsts[w][rows, :] + (1.0 - beta_one) * grad
            second_new = beta_two * seconds[w][rows, :] + (1.0 - beta_two) * grad * grad
            moment_v[w, 0, here, :] = first_new
            moment_v[w, 1, here, :] = second_new
            direction_v[w, here, :] = (
                first_new / bias_one / (jnp.sqrt(second_new / bias_two) + epsilon)
            ).astype(BF16)
            for m in range(2):
                send_out(moment_v.at[w, m, here], outs[2 + 2 * w + m], start, sems.at[w, i, m])
        for p in range(0, count, 2):
            both = pl.ds(p * 128, 256)
            step_v[w, both, :] = jnp.dot(
                direction_v[w, both, :], basis_ref[w], preferred_element_type=F32
            ).astype(BF16)
            for i in (p, p + 1):
                send_out(step_v.at[w, pl.ds(i * 128, 128)], outs[w], starts[i], sems.at[w, i, 2])
    for copy in pending:
        copy.wait()


def update(basis, moments, grads, places, before=()):
    rows, cols = moments[0].shape[0], basis.shape[2]
    count = len(places)
    return pl.pallas_call(
        functools.partial(update_kernel, places=places, before=len(before)),
        in_specs=[pl.BlockSpec(memory_space=pltpu.VMEM)] * (5 + count)
        + [pl.BlockSpec(memory_space=pl.ANY)] * len(before),
        out_specs=[pl.BlockSpec(memory_space=pl.ANY)] * 6,
        out_shape=[jax.ShapeDtypeStruct((rows, cols), BF16)] * 2
        + [jax.ShapeDtypeStruct((rows, R), F32)] * 4,
        scratch_shapes=[
            pltpu.VMEM((2, 128 * count, cols), BF16),
            pltpu.VMEM((2, 2, 128 * count, R), F32),
            pltpu.VMEM((2, 128 * count, R), BF16),
            pltpu.SemaphoreType.DMA((2, count, 3)),
        ],
        input_output_aliases={5 + count + n: n for n in range(len(before))},
        compiler_params=pltpu.CompilerParams(vmem_limit_bytes=16 * 2**20),
        cost_estimate=pl.CostEstimate(
            flops=count * 4 * 10**8, bytes_accessed=count * 10**6, transcendentals=0
        ),
        name="update_%d" % count,
    )(basis, *moments, *grads, *before)


def send(value, to):
    perm = []
    for source in range(128):
        x, zh, core, zl, y = (int(v) for v in np.unravel_index(source, SIZES))
        nx, nz, ncore, ny = to(x, zh * 2 + zl, core, y)
        nz %= 4
        target = int(
            np.ravel_multi_index((nx % 4, nz // 2, ncore, nz % 2, ny % 4), SIZES)
        )
        perm.append((source, target))
    return lax.ppermute(value, AXES, perm)


def swap_core(value):
    return lax.ppermute(value, "core", [(0, 1), (1, 0)])


def local(act, gate_cot, up_cot, seeds, gate_first, gate_second, up_first, up_second):
    zl = lax.axis_index("zl")

    def pool(value, k):
        return send(value, lambda x, z, c, y: (x + k, z, c, y) if c == 0 else (x, z, c, y + k))

    def across(value, k):
        return send(value, lambda x, z, c, y: (x, z, c, y + k) if c == 0 else (x + k, z, c, y))

    rows = act.shape[0]
    shares = rows_for(theirs_kernel, "theirs", rows, 5, act)
    near = pool(shares[4], 2)
    swapped = [swap_core(share) for share in shares[:4]]
    pairs = {
        k: rows_for(
            functools.partial(pair_kernel, k=k), "pair_%d" % k, 2 * rows, 1, act, swapped[k]
        )[0]
        for k in (1, 3)
    }
    pairs[2] = swapped[2]
    moved = {k: pool(pairs[k], k) for k in (1, 3, 2)}

    basis = basis_columns(seeds, FF // 16)

    late_seeds, pairs, swapped[0] = lax.optimization_barrier((seeds, pairs, swapped[0]))
    reduced = reduce_both(late_seeds, gate_cot, up_cot)
    pair = jnp.stack([reduced, swap_core(reduced)])
    pair, near = lax.optimization_barrier((pair, near))
    pooled = [pool(pair, k) for k in (1, 2)]
    last, moved[1], moved[3] = lax.optimization_barrier((pair, moved[1], moved[3]))
    pooled.append(pool(last, 3))

    others = [swapped[0], moved[1], near, moved[2], moved[3]]
    parts = partial_grads(act, others, [pair] + pooled)

    mine, basis = lax.optimization_barrier((parts[0], basis))
    here, away = sum_second([mine] + [across(parts[k], k) for k in (2, 1, 3)])

    done = here + send(away, lambda x, z, c, y: (x, z + 1, c, y))
    done = done + send(away, lambda x, z, c, y: (x, z - 1, c, y))
    done = done + send(here, lambda x, z, c, y: (x, z + 2, c, y))

    own = [done] + [
        send(done, lambda x, z, c, y, k=k: (x + k, z, c, y)) for k in range(1, 4)
    ]
    moments = (gate_first, gate_second, up_first, up_second)
    places = tuple((k, other) for k in range(4) for other in (False, True))
    grads = [swap_core(own[k]) if other else own[k] for k, other in places]
    outs = update(basis, moments, grads, places)
    gate_step, up_step, gfn, gsn, ufn, usn = outs
    return gate_step, up_step, gfn, gsn, ufn, usn


def solution(mesh):
    fine = Mesh(mesh.devices.reshape(SIZES), AXES)
    both = ("x", "zh", "core", "zl", "y")
    dp = ("x", "zh", "core")
    fsdp = ("zl", "y")
    return jax.shard_map(
        local,
        mesh=fine,
        in_specs=(P(both, None),) * 3 + (P(),) + (P(fsdp, None),) * 4,
        out_specs=(P(fsdp, dp),) * 2 + (P(fsdp, None),) * 4,
        check_vma=False,
    )
```

```python
import functools
import math

import jax
import jax.numpy as jnp
import numpy as np
from jax import lax
from jax.experimental import pallas as pl
from jax.experimental.pallas import tpu as pltpu
from jax.sharding import Mesh
from jax.sharding import PartitionSpec as P

FF = 28672
R = 128
TOKENS = 16384

beta_one = 0.9
beta_two = 0.95
bias_one = 1.0 - beta_one**10
bias_two = 1.0 - beta_two**10
epsilon = 1e-08

MIX_ONE = 668265261
MIX_TWO = 739982445
CENTRE = 32767.5 * 256.0
SCALE = float(np.float32(math.sqrt(3.0 / R))) * 2.0**-23

AXES = ("x", "zh", "core", "zl", "y")
SIZES = (4, 2, 2, 2, 4)

BF16 = jnp.bfloat16
F32 = jnp.float32


def finish(mixed):
    mixed = mixed ^ lax.shift_right_logical(mixed, 15)
    mixed = mixed * jnp.int32(MIX_TWO)
    mixed = mixed ^ lax.shift_right_logical(mixed, 12)
    level = (mixed & 0x00FFFF00).astype(F32)
    return ((level - CENTRE) * SCALE).astype(BF16)


def first_mix(local, low, seed):
    return (local ^ (seed & low)) * jnp.int32(MIX_ONE)


def base_mix(base, low, seed):
    return (base ^ (seed & ~low)) * jnp.int32(MIX_ONE)


CHUNK = 4096
TILE = 64
PIECE = 512
LOW = TILE * R - 1
FIRST, LAST = 0, 124


def tile_table(seed):
    local = lax.broadcasted_iota(jnp.int32, (TILE, R), 0) * R + lax.broadcasted_iota(
        jnp.int32, (TILE, R), 1
    )
    return first_mix(local, LOW, seed)


def basis_tile(table, seed, row):
    return finish(table + base_mix(row * R, LOW, seed))


def reduce_kernel(
    seed_ref, gate_hbm, up_hbm, out_ref, gate_v, up_v, even, odd, acc, sems
):
    chunks = FF // CHUNK
    hbm = (gate_hbm, up_hbm)
    held = (gate_v, up_v)

    def copy(w, i):
        cols = pl.ds(pl.multiple_of(i * CHUNK, CHUNK), CHUNK)
        return pltpu.make_async_copy(hbm[w].at[:, cols], held[w].at[:, cols], sems.at[w, i])

    for i in range(chunks):
        for w in range(2):
            copy(w, i).start()
    seeds = [seed_ref[0], seed_ref[1]]
    tables = [tile_table(seed) for seed in seeds]
    acc[...] = jnp.zeros_like(acc)
    tiles = [(w, t) for t in range(0, CHUNK, TILE) for w in range(2)]
    pieces = [(w, d) for d in range(0, CHUNK, PIECE) for w in range(2)]
    due = [
        max(0, min(len(pieces), -(-(n - FIRST) * len(pieces) // (LAST - FIRST))))
        for n in range(len(tiles))
    ]

    def step(i, fill, use):
        parts = [None, None]

        def multiply(w, d):
            if d == 0:
                copy(w, i - 1).wait()
            cols = pl.ds(pl.multiple_of((i - 1) * CHUNK + d, PIECE), PIECE)
            product = jnp.dot(
                held[w][:, cols], use[w, d : d + PIECE, :], preferred_element_type=F32
            )
            parts[w] = product if parts[w] is None else parts[w] + product

        if fill is None:
            for piece in pieces:
                multiply(*piece)
        else:
            done = 0
            for n, (w, t) in enumerate(tiles):
                for piece in pieces[done : due[n]]:
                    multiply(*piece)
                done = due[n]
                fill[w, t : t + TILE, :] = basis_tile(tables[w], seeds[w], i * CHUNK + t)
        for w in range(2):
            acc[w] += parts[w]

    for w, t in tiles:
        even[w, t : t + TILE, :] = basis_tile(tables[w], seeds[w], t)

    def body(k, carry):
        step(2 * k + 1, odd, even)
        step(2 * k + 2, even, odd)
        return carry

    lax.fori_loop(0, chunks // 2, body, 0)
    step(chunks, None, even)
    for w in range(2):
        out_ref[w] = acc[w].astype(BF16).astype(F32).T


def reduce_both(seeds, gate_cot, up_cot):
    rows = gate_cot.shape[0]
    return pl.pallas_call(
        reduce_kernel,
        in_specs=[
            pl.BlockSpec(memory_space=pltpu.SMEM),
            pl.BlockSpec(memory_space=pltpu.HBM),
            pl.BlockSpec(memory_space=pltpu.HBM),
        ],
        out_specs=pl.BlockSpec(memory_space=pltpu.VMEM),
        out_shape=jax.ShapeDtypeStruct((2, R, rows), F32),
        scratch_shapes=[
            pltpu.VMEM((rows, FF), BF16),
            pltpu.VMEM((rows, FF), BF16),
            pltpu.VMEM((2, CHUNK, R), BF16),
            pltpu.VMEM((2, CHUNK, R), BF16),
            pltpu.VMEM((2, rows, R), F32),
            pltpu.SemaphoreType.DMA((2, FF // CHUNK)),
        ],
        compiler_params=pltpu.CompilerParams(vmem_limit_bytes=50 * 2**20),
        cost_estimate=pl.CostEstimate(
            flops=20 * rows * FF * R, bytes_accessed=4 * rows * FF, transcendentals=0
        ),
        name="reduce_both",
    )(seeds, gate_cot, up_cot)


def place():
    return tuple(lax.axis_index(name).astype(jnp.int32) for name in AXES)


def pooled_columns(core, x, y, k, zl, j):
    zero = core == 0
    at = lax.rem(jnp.where(zero, x, y) + k, 4)
    a = zl * 4096 + j * jnp.where(zero, 1024, 128) + at * jnp.where(zero, 128, 1024)
    return pl.ds(pl.multiple_of(a + core * 512, 128), 128)


def theirs_kernel(act_ref, *outs):
    x, _, core, _, y = place()
    for i, out in enumerate(outs):
        owner, k = (1 - core, i) if i < 4 else (core, 2)
        for n in range(8):
            cols = pooled_columns(owner, x, y, k, n // 4, n % 4)
            out[:, n * 128 : (n + 1) * 128] = act_ref[:, cols].astype(F32)


def pair_kernel(act_ref, far_ref, out_ref, *, k):
    x, _, core, _, y = place()
    rows = act_ref.shape[0]
    for n in range(8):
        cols = pooled_columns(core, x, y, k, n // 4, n % 4)
        out_ref[:rows, n * 128 : (n + 1) * 128] = act_ref[:, cols].astype(F32)
    out_ref[rows:, :] = far_ref[...]


def rows_for(kernel, name, height, count, act, *far):
    return pl.pallas_call(
        kernel,
        in_specs=[pl.BlockSpec(memory_space=pltpu.VMEM)] * (1 + len(far)),
        out_specs=[pl.BlockSpec(memory_space=pltpu.VMEM)] * count,
        out_shape=[jax.ShapeDtypeStruct((height, 1024), F32)] * count,
        compiler_params=pltpu.CompilerParams(vmem_limit_bytes=10 * 2**20),
        cost_estimate=pl.CostEstimate(
            flops=height * 8192, bytes_accessed=6 * 2**20, transcendentals=0
        ),
        name=name,
    )(act, *far)


def grad_kernel(act_ref, *rest):
    x, _, core, _, y = place()
    second_at = jnp.where(core == 0, y, x)
    others = rest[:5]
    reds = rest[5:9]
    outs = rest[9:13]
    left = jnp.concatenate(
        [
            jnp.concatenate(
                [red[side, w].astype(BF16) for red in reds for side in range(2)], axis=1
            )
            for w in range(2)
        ],
        axis=0,
    )
    for k in range(4):
        j = lax.rem(second_at + k, 4)
        columns = []
        for zl in range(2):
            b = zl * 512 + j * 128
            columns.append(
                jnp.concatenate(
                    [act_ref[:, pooled_columns(core, x, y, 0, zl, j)]]
                    + [
                        other[:, pl.ds(pl.multiple_of(b, 128), 128)].astype(BF16)
                        for other in others
                    ],
                    axis=0,
                )
            )
        product = jnp.dot(
            left, jnp.concatenate(columns, axis=1), preferred_element_type=F32
        )
        for zl in range(2):
            for w in range(2):
                outs[k][w, zl] = product[
                    w * 128 : (w + 1) * 128, zl * 128 : (zl + 1) * 128
                ]


def partial_grads(act, others, reds):
    return pl.pallas_call(
        grad_kernel,
        in_specs=[pl.BlockSpec(memory_space=pltpu.VMEM)] * 10,
        out_specs=[pl.BlockSpec(memory_space=pltpu.VMEM)] * 4,
        out_shape=[jax.ShapeDtypeStruct((2, 2, 128, 128), F32)] * 4,
        compiler_params=pltpu.CompilerParams(vmem_limit_bytes=16 * 2**20),
        cost_estimate=pl.CostEstimate(
            flops=2 * 256 * 1024 * 1024, bytes_accessed=6 * 2**20, transcendentals=0
        ),
        name="partial_grads",
    )(act, *others, *reds)


def sum_kernel(*refs):
    zl = lax.axis_index("zl").astype(jnp.int32)
    here_ref, away_ref = refs[4:]
    for ref, at in ((here_ref, zl), (away_ref, 1 - zl)):
        for w in range(2):
            ref[w] = (refs[0][w, at] + refs[1][w, at]) + (refs[2][w, at] + refs[3][w, at])


def sum_second(parts):
    return pl.pallas_call(
        sum_kernel,
        in_specs=[pl.BlockSpec(memory_space=pltpu.VMEM)] * 4,
        out_specs=[pl.BlockSpec(memory_space=pltpu.VMEM)] * 2,
        out_shape=[jax.ShapeDtypeStruct((2, 128, 128), F32)] * 2,
        compiler_params=pltpu.CompilerParams(vmem_limit_bytes=4 * 2**20),
        cost_estimate=pl.CostEstimate(flops=10**6, bytes_accessed=10**6, transcendentals=0),
        name="sum_second",
    )(*parts)


def columns_kernel(seed_ref, out_ref):
    x, zh, core, _, _ = place()
    low = 128 * R - 1
    local = lax.broadcasted_iota(jnp.int32, (R, 128), 1) * R + lax.broadcasted_iota(
        jnp.int32, (R, 128), 0
    )
    count = out_ref.shape[2]
    base = ((x * 2 + zh) * 2 + core) * count
    for w in range(2):
        seed = seed_ref[w]
        table = first_mix(local, low, seed)
        for t in range(count // 128):
            start = base_mix((base + t * 128) * R, low, seed)
            out_ref[w, :, t * 128 : (t + 1) * 128] = finish(table + start)


def basis_columns(seeds, count):
    return pl.pallas_call(
        columns_kernel,
        in_specs=[pl.BlockSpec(memory_space=pltpu.SMEM)],
        out_specs=pl.BlockSpec(memory_space=pltpu.VMEM),
        out_shape=jax.ShapeDtypeStruct((2, R, count), BF16),
        compiler_params=pltpu.CompilerParams(vmem_limit_bytes=4 * 2**20),
        cost_estimate=pl.CostEstimate(
            flops=40 * R * count, bytes_accessed=4 * R * count, transcendentals=0
        ),
        name="basis_columns",
    )(seeds)


def update_kernel(basis_ref, gf_ref, gs_ref, uf_ref, us_ref, *rest, places, before):
    count = len(places)
    grads = rest[:count]
    outs = rest[count + before : count + before + 6]
    step_v, moment_v, direction_v, sems = rest[count + before + 6 :]
    firsts = (gf_ref, uf_ref)
    seconds = (gs_ref, us_ref)
    pending = []
    x, _, core, _, _ = place()
    starts = []
    for k, other in places:
        side = 1 - core if other else core
        starts.append(pl.multiple_of((side * 4 + lax.rem(x - k + 4, 4)) * 128, 128))

    def send_out(src, dst, start, sem):
        copy = pltpu.make_async_copy(src, dst.at[pl.ds(start, 128), :], sem)
        copy.start()
        pending.append(copy)

    for w in range(2):
        for i, start in enumerate(starts):
            rows = pl.ds(start, 128)
            here = pl.ds(i * 128, 128)
            grad = grads[i][w].T * (1.0 / TOKENS)
            first_new = beta_one * firsts[w][rows, :] + (1.0 - beta_one) * grad
            second_new = beta_two * seconds[w][rows, :] + (1.0 - beta_two) * grad * grad
            moment_v[w, 0, here, :] = first_new
            moment_v[w, 1, here, :] = second_new
            direction_v[w, here, :] = (
                first_new / bias_one / (jnp.sqrt(second_new / bias_two) + epsilon)
            ).astype(BF16)
            for m in range(2):
                send_out(moment_v.at[w, m, here], outs[2 + 2 * w + m], start, sems.at[w, i, m])
        for p in range(0, count, 2):
            both = pl.ds(p * 128, 256)
            step_v[w, both, :] = jnp.dot(
                direction_v[w, both, :], basis_ref[w], preferred_element_type=F32
            ).astype(BF16)
            for i in (p, p + 1):
                send_out(step_v.at[w, pl.ds(i * 128, 128)], outs[w], starts[i], sems.at[w, i, 2])
    for copy in pending:
        copy.wait()


def update(basis, moments, grads, places, before=()):
    rows, cols = moments[0].shape[0], basis.shape[2]
    count = len(places)
    return pl.pallas_call(
        functools.partial(update_kernel, places=places, before=len(before)),
        in_specs=[pl.BlockSpec(memory_space=pltpu.VMEM)] * (5 + count)
        + [pl.BlockSpec(memory_space=pl.ANY)] * len(before),
        out_specs=[pl.BlockSpec(memory_space=pl.ANY)] * 6,
        out_shape=[jax.ShapeDtypeStruct((rows, cols), BF16)] * 2
        + [jax.ShapeDtypeStruct((rows, R), F32)] * 4,
        scratch_shapes=[
            pltpu.VMEM((2, 128 * count, cols), BF16),
            pltpu.VMEM((2, 2, 128 * count, R), F32),
            pltpu.VMEM((2, 128 * count, R), BF16),
            pltpu.SemaphoreType.DMA((2, count, 3)),
        ],
        input_output_aliases={5 + count + n: n for n in range(len(before))},
        compiler_params=pltpu.CompilerParams(vmem_limit_bytes=16 * 2**20),
        cost_estimate=pl.CostEstimate(
            flops=count * 4 * 10**8, bytes_accessed=count * 10**6, transcendentals=0
        ),
        name="update_%d" % count,
    )(basis, *moments, *grads, *before)


def send(value, to):
    perm = []
    for source in range(128):
        x, zh, core, zl, y = (int(v) for v in np.unravel_index(source, SIZES))
        nx, nz, ncore, ny = to(x, zh * 2 + zl, core, y)
        nz %= 4
        target = int(
            np.ravel_multi_index((nx % 4, nz // 2, ncore, nz % 2, ny % 4), SIZES)
        )
        perm.append((source, target))
    return lax.ppermute(value, AXES, perm)


def swap_core(value):
    return lax.ppermute(value, "core", [(0, 1), (1, 0)])


def local(act, gate_cot, up_cot, seeds, gate_first, gate_second, up_first, up_second):
    zl = lax.axis_index("zl")

    def pool(value, k):
        return send(value, lambda x, z, c, y: (x + k, z, c, y) if c == 0 else (x, z, c, y + k))

    def across(value, k):
        return send(value, lambda x, z, c, y: (x, z, c, y + k) if c == 0 else (x + k, z, c, y))

    rows = act.shape[0]
    shares = rows_for(theirs_kernel, "theirs", rows, 5, act)
    near = pool(shares[4], 2)
    swapped = [swap_core(share) for share in shares[:4]]
    pairs = {
        k: rows_for(
            functools.partial(pair_kernel, k=k), "pair_%d" % k, 2 * rows, 1, act, swapped[k]
        )[0]
        for k in (1, 3)
    }
    pairs[2] = swapped[2]
    moved = {k: pool(pairs[k], k) for k in (1, 3, 2)}

    basis = basis_columns(seeds, FF // 16)

    late_seeds, pairs, swapped[0] = lax.optimization_barrier((seeds, pairs, swapped[0]))
    reduced = reduce_both(late_seeds, gate_cot, up_cot)
    pair = jnp.stack([reduced, swap_core(reduced)])
    pair, near = lax.optimization_barrier((pair, near))
    pooled = [pool(pair, k) for k in (1, 2)]
    last, moved[1], moved[3] = lax.optimization_barrier((pair, moved[1], moved[3]))
    pooled.append(pool(last, 3))

    others = [swapped[0], moved[1], near, moved[2], moved[3]]
    parts = partial_grads(act, others, [pair] + pooled)

    mine, basis = lax.optimization_barrier((parts[0], basis))
    here, away = sum_second([mine] + [across(parts[k], k) for k in (2, 1, 3)])

    done = here + send(away, lambda x, z, c, y: (x, z + 1, c, y))
    done = done + send(away, lambda x, z, c, y: (x, z - 1, c, y))
    done = done + send(here, lambda x, z, c, y: (x, z + 2, c, y))

    own = [done] + [
        send(done, lambda x, z, c, y, k=k: (x + k, z, c, y)) for k in range(1, 4)
    ]
    moments = (gate_first, gate_second, up_first, up_second)
    places = tuple((k, other) for k in range(4) for other in (False, True))
    grads = [swap_core(own[k]) if other else own[k] for k, other in places]
    outs = update(basis, moments, grads, places)
    gate_step, up_step, gfn, gsn, ufn, usn = outs
    return gate_step, up_step, gfn, gsn, ufn, usn


def solution(mesh):
    fine = Mesh(mesh.devices.reshape(SIZES), AXES)
    both = ("x", "zh", "core", "zl", "y")
    dp = ("x", "zh", "core")
    fsdp = ("zl", "y")
    return jax.shard_map(
        local,
        mesh=fine,
        in_specs=(P(both, None),) * 3 + (P(),) + (P(fsdp, None),) * 4,
        out_specs=(P(fsdp, dp),) * 2 + (P(fsdp, None),) * 4,
        check_vma=False,
    )
```

```python
import functools
import math

import jax
import jax.numpy as jnp
import numpy as np
from jax import lax
from jax.experimental import pallas as pl
from jax.experimental.pallas import tpu as pltpu
from jax.sharding import Mesh
from jax.sharding import PartitionSpec as P

FF = 28672
R = 128
TOKENS = 16384

beta_one = 0.9
beta_two = 0.95
bias_one = 1.0 - beta_one**10
bias_two = 1.0 - beta_two**10
epsilon = 1e-08

MIX_ONE = 668265261
MIX_TWO = 739982445
CENTRE = 32767.5 * 256.0
SCALE = float(np.float32(math.sqrt(3.0 / R))) * 2.0**-23

AXES = ("x", "zh", "core", "zl", "y")
SIZES = (4, 2, 2, 2, 4)

BF16 = jnp.bfloat16
F32 = jnp.float32


def finish(mixed):
    mixed = mixed ^ lax.shift_right_logical(mixed, 15)
    mixed = mixed * jnp.int32(MIX_TWO)
    mixed = mixed ^ lax.shift_right_logical(mixed, 12)
    level = (mixed & 0x00FFFF00).astype(F32)
    return ((level - CENTRE) * SCALE).astype(BF16)


def first_mix(local, low, seed):
    return (local ^ (seed & low)) * jnp.int32(MIX_ONE)


def base_mix(base, low, seed):
    return (base ^ (seed & ~low)) * jnp.int32(MIX_ONE)


CHUNK = 4096
TILE = 64
PIECE = 512
LOW = TILE * R - 1
FIRST, LAST = 0, 124


def tile_table(seed):
    local = lax.broadcasted_iota(jnp.int32, (TILE, R), 0) * R + lax.broadcasted_iota(
        jnp.int32, (TILE, R), 1
    )
    return first_mix(local, LOW, seed)


def basis_tile(table, seed, row):
    return finish(table + base_mix(row * R, LOW, seed))


def reduce_kernel(
    seed_ref, gate_hbm, up_hbm, out_ref, gate_v, up_v, even, odd, acc, sems
):
    chunks = FF // CHUNK
    hbm = (gate_hbm, up_hbm)
    held = (gate_v, up_v)

    def copy(w, i):
        cols = pl.ds(pl.multiple_of(i * CHUNK, CHUNK), CHUNK)
        return pltpu.make_async_copy(hbm[w].at[:, cols], held[w].at[:, cols], sems.at[w, i])

    for i in range(chunks):
        for w in range(2):
            copy(w, i).start()
    seeds = [seed_ref[0], seed_ref[1]]
    tables = [tile_table(seed) for seed in seeds]
    acc[...] = jnp.zeros_like(acc)
    tiles = [(w, t) for t in range(0, CHUNK, TILE) for w in range(2)]
    pieces = [(w, d) for d in range(0, CHUNK, PIECE) for w in range(2)]
    due = [
        max(0, min(len(pieces), -(-(n - FIRST) * len(pieces) // (LAST - FIRST))))
        for n in range(len(tiles))
    ]

    def step(i, fill, use):
        parts = [None, None]

        def multiply(w, d):
            if d == 0:
                copy(w, i - 1).wait()
            cols = pl.ds(pl.multiple_of((i - 1) * CHUNK + d, PIECE), PIECE)
            product = jnp.dot(
                held[w][:, cols], use[w, d : d + PIECE, :], preferred_element_type=F32
            )
            parts[w] = product if parts[w] is None else parts[w] + product

        if fill is None:
            for piece in pieces:
                multiply(*piece)
        else:
            done = 0
            for n, (w, t) in enumerate(tiles):
                for piece in pieces[done : due[n]]:
                    multiply(*piece)
                done = due[n]
                fill[w, t : t + TILE, :] = basis_tile(tables[w], seeds[w], i * CHUNK + t)
        for w in range(2):
            acc[w] += parts[w]

    for w, t in tiles:
        even[w, t : t + TILE, :] = basis_tile(tables[w], seeds[w], t)

    def body(k, carry):
        step(2 * k + 1, odd, even)
        step(2 * k + 2, even, odd)
        return carry

    lax.fori_loop(0, chunks // 2, body, 0)
    step(chunks, None, even)
    for w in range(2):
        out_ref[w] = acc[w].astype(BF16).astype(F32).T


def reduce_both(seeds, gate_cot, up_cot):
    rows = gate_cot.shape[0]
    return pl.pallas_call(
        reduce_kernel,
        in_specs=[
            pl.BlockSpec(memory_space=pltpu.SMEM),
            pl.BlockSpec(memory_space=pltpu.HBM),
            pl.BlockSpec(memory_space=pltpu.HBM),
        ],
        out_specs=pl.BlockSpec(memory_space=pltpu.VMEM),
        out_shape=jax.ShapeDtypeStruct((2, R, rows), F32),
        scratch_shapes=[
            pltpu.VMEM((rows, FF), BF16),
            pltpu.VMEM((rows, FF), BF16),
            pltpu.VMEM((2, CHUNK, R), BF16),
            pltpu.VMEM((2, CHUNK, R), BF16),
            pltpu.VMEM((2, rows, R), F32),
            pltpu.SemaphoreType.DMA((2, FF // CHUNK)),
        ],
        compiler_params=pltpu.CompilerParams(vmem_limit_bytes=50 * 2**20),
        cost_estimate=pl.CostEstimate(
            flops=20 * rows * FF * R, bytes_accessed=4 * rows * FF, transcendentals=0
        ),
        name="reduce_both",
    )(seeds, gate_cot, up_cot)


def place():
    return tuple(lax.axis_index(name).astype(jnp.int32) for name in AXES)


def pooled_columns(core, x, y, k, zl, j):
    zero = core == 0
    at = lax.rem(jnp.where(zero, x, y) + k, 4)
    a = zl * 4096 + j * jnp.where(zero, 1024, 128) + at * jnp.where(zero, 128, 1024)
    return pl.ds(pl.multiple_of(a + core * 512, 128), 128)


def theirs_kernel(act_ref, *outs):
    x, _, core, _, y = place()
    for i, out in enumerate(outs):
        owner, k = (1 - core, i) if i < 4 else (core, 2)
        for n in range(8):
            cols = pooled_columns(owner, x, y, k, n // 4, n % 4)
            out[:, n * 128 : (n + 1) * 128] = act_ref[:, cols].astype(F32)


def pair_kernel(act_ref, far_ref, out_ref, *, k):
    x, _, core, _, y = place()
    rows = act_ref.shape[0]
    for n in range(8):
        cols = pooled_columns(core, x, y, k, n // 4, n % 4)
        out_ref[:rows, n * 128 : (n + 1) * 128] = act_ref[:, cols].astype(F32)
    out_ref[rows:, :] = far_ref[...]


def rows_for(kernel, name, height, count, act, *far):
    return pl.pallas_call(
        kernel,
        in_specs=[pl.BlockSpec(memory_space=pltpu.VMEM)] * (1 + len(far)),
        out_specs=[pl.BlockSpec(memory_space=pltpu.VMEM)] * count,
        out_shape=[jax.ShapeDtypeStruct((height, 1024), F32)] * count,
        compiler_params=pltpu.CompilerParams(vmem_limit_bytes=10 * 2**20),
        cost_estimate=pl.CostEstimate(
            flops=height * 8192, bytes_accessed=6 * 2**20, transcendentals=0
        ),
        name=name,
    )(act, *far)


def grad_kernel(act_ref, *rest):
    x, _, core, _, y = place()
    second_at = jnp.where(core == 0, y, x)
    others = rest[:5]
    reds = rest[5:9]
    outs = rest[9:13]
    left = jnp.concatenate(
        [
            jnp.concatenate(
                [red[side, w].astype(BF16) for red in reds for side in range(2)], axis=1
            )
            for w in range(2)
        ],
        axis=0,
    )
    for k in range(4):
        j = lax.rem(second_at + k, 4)
        columns = []
        for zl in range(2):
            b = zl * 512 + j * 128
            columns.append(
                jnp.concatenate(
                    [act_ref[:, pooled_columns(core, x, y, 0, zl, j)]]
                    + [
                        other[:, pl.ds(pl.multiple_of(b, 128), 128)].astype(BF16)
                        for other in others
                    ],
                    axis=0,
                )
            )
        product = jnp.dot(
            left, jnp.concatenate(columns, axis=1), preferred_element_type=F32
        )
        for zl in range(2):
            for w in range(2):
                outs[k][w, zl] = product[
                    w * 128 : (w + 1) * 128, zl * 128 : (zl + 1) * 128
                ]


def partial_grads(act, others, reds):
    return pl.pallas_call(
        grad_kernel,
        in_specs=[pl.BlockSpec(memory_space=pltpu.VMEM)] * 10,
        out_specs=[pl.BlockSpec(memory_space=pltpu.VMEM)] * 4,
        out_shape=[jax.ShapeDtypeStruct((2, 2, 128, 128), F32)] * 4,
        compiler_params=pltpu.CompilerParams(vmem_limit_bytes=16 * 2**20),
        cost_estimate=pl.CostEstimate(
            flops=2 * 256 * 1024 * 1024, bytes_accessed=6 * 2**20, transcendentals=0
        ),
        name="partial_grads",
    )(act, *others, *reds)


def sum_kernel(*refs):
    zl = lax.axis_index("zl").astype(jnp.int32)
    here_ref, away_ref = refs[4:]
    for ref, at in ((here_ref, zl), (away_ref, 1 - zl)):
        for w in range(2):
            ref[w] = (refs[0][w, at] + refs[1][w, at]) + (refs[2][w, at] + refs[3][w, at])


def sum_second(parts):
    return pl.pallas_call(
        sum_kernel,
        in_specs=[pl.BlockSpec(memory_space=pltpu.VMEM)] * 4,
        out_specs=[pl.BlockSpec(memory_space=pltpu.VMEM)] * 2,
        out_shape=[jax.ShapeDtypeStruct((2, 128, 128), F32)] * 2,
        compiler_params=pltpu.CompilerParams(vmem_limit_bytes=4 * 2**20),
        cost_estimate=pl.CostEstimate(flops=10**6, bytes_accessed=10**6, transcendentals=0),
        name="sum_second",
    )(*parts)


def columns_kernel(seed_ref, out_ref):
    x, zh, core, _, _ = place()
    low = 128 * R - 1
    local = lax.broadcasted_iota(jnp.int32, (R, 128), 1) * R + lax.broadcasted_iota(
        jnp.int32, (R, 128), 0
    )
    count = out_ref.shape[2]
    base = ((x * 2 + zh) * 2 + core) * count
    for w in range(2):
        seed = seed_ref[w]
        table = first_mix(local, low, seed)
        for t in range(count // 128):
            start = base_mix((base + t * 128) * R, low, seed)
            out_ref[w, :, t * 128 : (t + 1) * 128] = finish(table + start)


def basis_columns(seeds, count):
    return pl.pallas_call(
        columns_kernel,
        in_specs=[pl.BlockSpec(memory_space=pltpu.SMEM)],
        out_specs=pl.BlockSpec(memory_space=pltpu.VMEM),
        out_shape=jax.ShapeDtypeStruct((2, R, count), BF16),
        compiler_params=pltpu.CompilerParams(vmem_limit_bytes=4 * 2**20),
        cost_estimate=pl.CostEstimate(
            flops=40 * R * count, bytes_accessed=4 * R * count, transcendentals=0
        ),
        name="basis_columns",
    )(seeds)


def update_kernel(basis_ref, gf_ref, gs_ref, uf_ref, us_ref, *rest, places, before):
    count = len(places)
    grads = rest[:count]
    outs = rest[count + before : count + before + 6]
    step_v, moment_v, direction_v, sems = rest[count + before + 6 :]
    firsts = (gf_ref, uf_ref)
    seconds = (gs_ref, us_ref)
    pending = []
    x, _, core, _, _ = place()
    starts = []
    for k, other in places:
        side = 1 - core if other else core
        starts.append(pl.multiple_of((side * 4 + lax.rem(x - k + 4, 4)) * 128, 128))

    def send_out(src, dst, start, sem):
        copy = pltpu.make_async_copy(src, dst.at[pl.ds(start, 128), :], sem)
        copy.start()
        pending.append(copy)

    for w in range(2):
        for i, start in enumerate(starts):
            rows = pl.ds(start, 128)
            here = pl.ds(i * 128, 128)
            grad = grads[i][w].T * (1.0 / TOKENS)
            first_new = beta_one * firsts[w][rows, :] + (1.0 - beta_one) * grad
            second_new = beta_two * seconds[w][rows, :] + (1.0 - beta_two) * grad * grad
            moment_v[w, 0, here, :] = first_new
            moment_v[w, 1, here, :] = second_new
            direction_v[w, here, :] = (
                first_new / bias_one / (jnp.sqrt(second_new / bias_two) + epsilon)
            ).astype(BF16)
            for m in range(2):
                send_out(moment_v.at[w, m, here], outs[2 + 2 * w + m], start, sems.at[w, i, m])
        for p in range(0, count, 2):
            both = pl.ds(p * 128, 256)
            step_v[w, both, :] = jnp.dot(
                direction_v[w, both, :], basis_ref[w], preferred_element_type=F32
            ).astype(BF16)
            for i in (p, p + 1):
                send_out(step_v.at[w, pl.ds(i * 128, 128)], outs[w], starts[i], sems.at[w, i, 2])
    for copy in pending:
        copy.wait()


def update(basis, moments, grads, places, before=()):
    rows, cols = moments[0].shape[0], basis.shape[2]
    count = len(places)
    return pl.pallas_call(
        functools.partial(update_kernel, places=places, before=len(before)),
        in_specs=[pl.BlockSpec(memory_space=pltpu.VMEM)] * (5 + count)
        + [pl.BlockSpec(memory_space=pl.ANY)] * len(before),
        out_specs=[pl.BlockSpec(memory_space=pl.ANY)] * 6,
        out_shape=[jax.ShapeDtypeStruct((rows, cols), BF16)] * 2
        + [jax.ShapeDtypeStruct((rows, R), F32)] * 4,
        scratch_shapes=[
            pltpu.VMEM((2, 128 * count, cols), BF16),
            pltpu.VMEM((2, 2, 128 * count, R), F32),
            pltpu.VMEM((2, 128 * count, R), BF16),
            pltpu.SemaphoreType.DMA((2, count, 3)),
        ],
        input_output_aliases={5 + count + n: n for n in range(len(before))},
        compiler_params=pltpu.CompilerParams(vmem_limit_bytes=16 * 2**20),
        cost_estimate=pl.CostEstimate(
            flops=count * 4 * 10**8, bytes_accessed=count * 10**6, transcendentals=0
        ),
        name="update_%d" % count,
    )(basis, *moments, *grads, *before)


def send(value, to):
    perm = []
    for source in range(128):
        x, zh, core, zl, y = (int(v) for v in np.unravel_index(source, SIZES))
        nx, nz, ncore, ny = to(x, zh * 2 + zl, core, y)
        nz %= 4
        target = int(
            np.ravel_multi_index((nx % 4, nz // 2, ncore, nz % 2, ny % 4), SIZES)
        )
        perm.append((source, target))
    return lax.ppermute(value, AXES, perm)


def swap_core(value):
    return lax.ppermute(value, "core", [(0, 1), (1, 0)])


def local(act, gate_cot, up_cot, seeds, gate_first, gate_second, up_first, up_second):
    zl = lax.axis_index("zl")

    def pool(value, k):
        return send(value, lambda x, z, c, y: (x + k, z, c, y) if c == 0 else (x, z, c, y + k))

    def across(value, k):
        return send(value, lambda x, z, c, y: (x, z, c, y + k) if c == 0 else (x + k, z, c, y))

    rows = act.shape[0]
    shares = rows_for(theirs_kernel, "theirs", rows, 5, act)
    near = pool(shares[4], 2)
    swapped = [swap_core(share) for share in shares[:4]]
    pairs = {
        k: rows_for(
            functools.partial(pair_kernel, k=k), "pair_%d" % k, 2 * rows, 1, act, swapped[k]
        )[0]
        for k in (1, 3)
    }
    pairs[2] = swapped[2]
    moved = {k: pool(pairs[k], k) for k in (1, 3, 2)}

    basis = basis_columns(seeds, FF // 16)

    late_seeds, pairs, swapped[0] = lax.optimization_barrier((seeds, pairs, swapped[0]))
    reduced = reduce_both(late_seeds, gate_cot, up_cot)
    pair = jnp.stack([reduced, swap_core(reduced)])
    pair, near = lax.optimization_barrier((pair, near))
    pooled = [pool(pair, k) for k in (1, 2)]
    last, moved[1], moved[3] = lax.optimization_barrier((pair, moved[1], moved[3]))
    pooled.append(pool(last, 3))

    others = [swapped[0], moved[1], near, moved[2], moved[3]]
    parts = partial_grads(act, others, [pair] + pooled)

    mine, basis = lax.optimization_barrier((parts[0], basis))
    here, away = sum_second([mine] + [across(parts[k], k) for k in (2, 1, 3)])

    done = here + send(away, lambda x, z, c, y: (x, z + 1, c, y))
    done = done + send(away, lambda x, z, c, y: (x, z - 1, c, y))
    done = done + send(here, lambda x, z, c, y: (x, z + 2, c, y))

    own = [done] + [
        send(done, lambda x, z, c, y, k=k: (x + k, z, c, y)) for k in range(1, 4)
    ]
    moments = (gate_first, gate_second, up_first, up_second)
    places = tuple((k, other) for k in (0, 2, 3, 1) for other in (False, True))
    grads = [swap_core(own[k]) if other else own[k] for k, other in places]
    outs = update(basis, moments, grads, places)
    gate_step, up_step, gfn, gsn, ufn, usn = outs
    return gate_step, up_step, gfn, gsn, ufn, usn


def solution(mesh):
    fine = Mesh(mesh.devices.reshape(SIZES), AXES)
    both = ("x", "zh", "core", "zl", "y")
    dp = ("x", "zh", "core")
    fsdp = ("zl", "y")
    return jax.shard_map(
        local,
        mesh=fine,
        in_specs=(P(both, None),) * 3 + (P(),) + (P(fsdp, None),) * 4,
        out_specs=(P(fsdp, dp),) * 2 + (P(fsdp, None),) * 4,
        check_vma=False,
    )
```
